32 devices in a mesh: grp: 2 (over x), row: 16 (over z, y, core).
Axes of the slice: x: 2, y: 2, z: 4, core: 2. Of those that a mesh axis runs over, the one named last changes fastest.
Arguments:
- greens: bfloat16 [8192, 16384], P(('grp', 'row')), parts along dimension 0, may hold values from -0.0625 to 0.0625
- track_id: int32 [8192], P(('grp', 'row')), parts along dimension 0, may hold values from 0 to 7
- sigma_inv: float32 [16], P('grp'), parts along dimension 0, may hold values from 1 to 10
- sketch: float32 [192, 128, 128], P('grp', 'row'), parts along dimension 0, may hold values from -6 to 6
Outputs:
- range_basis: float32 [8192, 96], P(('grp', 'row')), parts along dimension 0
- coefficients: float32 [256, 128, 96], P(('grp', 'row')), parts along dimension 0
The draws below stay inside these ranges and needn't reach their ends.
There are 2 independent parts, one for each index of `grp`. The reference program is written for one: setup_inputs(seed, part) draws one part's arguments, and reference() takes and returns one part's arrays. A program takes and returns all parts, laid end to end along the dimension named above; each array names one. Nothing has to cross between parts.
All inputs are finite; a program needn't handle non-finite values.
Results may differ from the reference program's by a relative error of at most 0.011.
Values may be sent and summed in bfloat16 or wider, within the bound.
A program may use at most 128 MiB of HBM per device.

```python
import math
import jax
import jax.numpy as jnp
from jax import lax

NDIP = 128
NSTRIKE = 128
SKETCH = 96
NTRACK = 8
SWEEPS = 4
ROWS = 4096
PARAMS = 16384


def draw_sketch(key, part):
    common_key = jax.random.fold_in(key, 11)
    column_key = jax.random.fold_in(key, 23)
    common_part = jax.random.normal(common_key, (1, NDIP, NSTRIKE), jnp.float32)
    column_part = jax.random.normal(column_key, (SKETCH, NDIP, NSTRIKE), jnp.float32)
    return jnp.clip(0.95 * common_part + 0.3 * column_part, -6.0, 6.0)


def plant(entries, own_key, smallest, high):
    index_at = [jax.random.randint(jax.random.fold_in(own_key, axis), (), 0, length) for axis, length in enumerate(entries.shape)]
    main_axis = entries.shape.index(max(entries.shape))
    next_to = index_at[:main_axis] + [(index_at[main_axis] + 1) % entries.shape[main_axis]] + index_at[main_axis + 1:]
    return entries.at[tuple(index_at)].set(smallest).at[tuple(next_to)].set(high)


def spiked(drawn, key, source, target, shards_of, factor):
    owner, partner = [(jnp.arange(drawn.shape[position]) // (drawn.shape[position] // shards_of)).reshape([-1 if axis == position else 1 for axis in range(drawn.ndim)]) for position in (source, target)]
    chosen = jax.random.permutation(key, shards_of)[partner]
    strong = (owner == chosen) | (owner == (partner + shards_of // 2) % shards_of)
    return jnp.where(strong, factor * drawn, drawn)


def level_of(rng, shape, split, least, top_value):
    loudness, own = 1.0, jax.random.fold_in(rng, 6)
    for dim, parts in split:
        draws = jnp.exp(jax.random.uniform(jax.random.fold_in(own, dim), (parts,), jnp.float32, least / len(split), top_value / len(split)))
        loudness = loudness * jnp.repeat(draws, shape[dim] // parts).reshape([-1 if axis == dim else 1 for axis in range(len(shape))])
    return loudness


def gaussian_with(own_key, extent, spread, bound, pieces, heavy, kind=jnp.bfloat16):
    values = spread * jax.random.normal(own_key, extent, jnp.float32)
    if pieces:
        values = values * level_of(own_key, extent, pieces, -0.22, 0.18)
    return jnp.clip(spiked(values, jax.random.fold_in(own_key, 3), *heavy), -bound, bound).astype(kind)


def setup_inputs(seed: int = 0, part: int = 0) -> dict:
    key_of = jax.random.split(jax.random.key(seed), 5)
    part_splits = jax.random.split(jax.random.fold_in(key_of[4], part), 5)
    greens = gaussian_with(part_splits[0], (ROWS, PARAMS), PARAMS ** -0.5, 0.0625, ((0, 16),), (0, 1, 16, 2.0))
    track_id = plant(jax.random.randint(part_splits[1], (ROWS,), 0, NTRACK), jax.random.fold_in(part_splits[1], 1), 0, NTRACK - 1).astype(jnp.int32)
    sigma_inv = jnp.clip(jnp.exp(jax.random.uniform(part_splits[2], (NTRACK,), jnp.float32, math.log(1.0), math.log(10.0))), 1.0, 10.0)
    sketch = draw_sketch(jax.random.fold_in(jax.random.fold_in(key_of[4], part), 71), part)
    return dict(greens=greens, track_id=track_id, sigma_inv=sigma_inv, sketch=sketch)


smoothing = 0.24

def smooth_once(field):
    padded = jnp.pad(field, ((0, 0), (1, 1), (1, 1)))
    beside_all = padded[:, 2:, 1:-1] + padded[:, :-2, 1:-1] + padded[:, 1:-1, 2:] + padded[:, 1:-1, :-2]
    return field + smoothing * (beside_all - 4.0 * field)

def orthonormalize(sketched):
    gram_matrix = jnp.dot(sketched.T, sketched, precision=lax.Precision.HIGHEST) / ROWS
    factor = jnp.linalg.cholesky(gram_matrix)
    return lax.linalg.triangular_solve(factor, sketched, left_side=False, lower=True, transpose_a=True)

def reference(greens, track_id, sigma_inv, sketch):
    groups = jnp.arange(NTRACK, dtype=jnp.int32)
    onehot = (track_id[:, None] == groups[None, :]).astype(jnp.float32)
    weights = jnp.dot(onehot, sigma_inv, precision=lax.Precision.HIGHEST)
    field = sketch
    for sweep_index in range(SWEEPS):
        field = smooth_once(field)
    omega = field.reshape(SKETCH, PARAMS).astype(jnp.bfloat16)
    first = lax.dot_general(greens.astype(jnp.float32), omega.astype(jnp.float32), (((1,), (1,)), ((), ())), preferred_element_type=jnp.float32)
    basis_one = orthonormalize(first * weights[:, None])
    weighted_one = (basis_one * weights[:, None]).astype(jnp.bfloat16)
    row_scale = 1.0 / jnp.sqrt(jnp.float32(ROWS))
    back = lax.dot_general(greens.astype(jnp.float32), weighted_one.astype(jnp.float32), (((0,), (0,)), ((), ())), preferred_element_type=jnp.float32)
    back = (back * row_scale).astype(jnp.bfloat16)
    second = jnp.dot(greens.astype(jnp.float32), back.astype(jnp.float32), preferred_element_type=jnp.float32)
    range_basis = orthonormalize(second * weights[:, None])
    weighted_two = (range_basis * weights[:, None]).astype(jnp.bfloat16)
    projected = lax.dot_general(greens.astype(jnp.float32), weighted_two.astype(jnp.float32), (((0,), (0,)), ((), ())), preferred_element_type=jnp.float32)
    coefficients = (projected * row_scale).reshape(NDIP, NSTRIKE, SKETCH)
    return (range_basis, coefficients)
```

```python
import functools
import jax
import jax.numpy as jnp
from jax import lax
from jax.experimental import pallas as pl
from jax.experimental.pallas import tpu as pltpu
from jax.sharding import PartitionSpec as P

SWEEPS = 4
smoothing = 0.24
VMEM_LIMIT = 52 * 1024 * 1024


def smooth(sketch):
    length = sketch.shape[1]
    count = lax.axis_size("row")
    before, after = [], []
    for hop in range(1, -(-SWEEPS // length) + 1):
        take = min(length, SWEEPS - (hop - 1) * length)
        up = [(i, i + hop) for i in range(count - hop)]
        down = [(j, i) for i, j in up]
        before.insert(0, lax.ppermute(sketch[:, length - take :], "row", up))
        after.append(lax.ppermute(sketch[:, :take], "row", down))
    field = jnp.concatenate(before + [sketch] + after, axis=1)
    first_row = lax.axis_index("row") * length - SWEEPS
    for sweep in range(1, SWEEPS + 1):
        padded = jnp.pad(field, ((0, 0), (0, 0), (1, 1)))
        centre = field[:, 1:-1]
        beside_all = (
            padded[:, 2:, 1:-1] + padded[:, :-2, 1:-1] + padded[:, 1:-1, 2:] + padded[:, 1:-1, :-2]
        )
        field = centre + smoothing * (beside_all - 4.0 * centre)
        if sweep < SWEEPS:
            rows = first_row + sweep + jnp.arange(field.shape[1], dtype=jnp.int32)
            inside = (rows >= 0) & (rows < length * count)
            field = jnp.where(inside[None, :, None], field, 0.0)
    return field


class Place:
    def __init__(self, n):
        self.n = n
        self.steps = n.bit_length() - 1
        self.me = lax.axis_index("row")
        rest = list(range(1, self.steps))
        self.orders = ([0] + rest, [0] + rest[1:] + rest[:1])

    def bit(self, k, of=None):
        return lax.rem(lax.div(self.me if of is None else of, 2**k), 2)

    def partner(self, k):
        return {"row": self.me + 2**k * (1 - 2 * self.bit(k))}

    def slot(self, block, order):
        return sum(self.bit(k, block) * 2 ** (self.steps - 1 - i) for i, k in enumerate(order))

    def greet(self):
        barrier = pltpu.get_barrier_semaphore()
        for k in range(self.steps):
            pl.semaphore_signal(
                barrier, inc=1, device_id=self.partner(k), device_id_type=pl.DeviceIdType.MESH
            )
        pl.semaphore_wait(barrier, self.steps)

    def send(self, source, target, k, sems, *at):
        copy = pltpu.make_async_remote_copy(
            src_ref=source,
            dst_ref=target,
            send_sem=sems.at[(0, *at)],
            recv_sem=sems.at[(1, *at)],
            device_id=self.partner(k),
            device_id_type=pl.DeviceIdType.MESH,
        )
        copy.start()
        return copy


def reduce_scatter(place, g_ref, w_ref, acc, wide, outgo, income, sems):
    n, depth = place.n, acc[0].shape[1]
    width = acc[0].shape[2]
    own = place.bit(0)

    def produce(core):
        def body(j, carry):
            block = 2 * j + core
            columns = pl.ds(pl.multiple_of(block * width, 128), width)
            part = jnp.dot(w_ref[...], g_ref[:, columns], preferred_element_type=jnp.float32)
            for s in range(2):
                acc[s][place.slot(block, place.orders[s])] = part[s * depth : (s + 1) * depth]
            return carry

        lax.fori_loop(0, n // 2, body, 0)

    produce(1 - own)
    half = n // 2
    copies = [
        place.send(acc[s].at[pl.ds((1 - own) * half, half)], wide[s], 0, sems, 0, s)
        for s in range(2)
    ]
    produce(own)
    base = [own * half, own * half]
    arrived, arrived_at, at = wide, 0, 0
    for step in range(1, place.steps):
        half = n >> (step + 1)
        for s in range(2):
            k = place.orders[s][step]
            mine = place.bit(k)
            copies[s].wait()

            def pack(i, carry):
                j = (1 - mine) * half + i
                total = acc[s][base[s] + j] + arrived[s][arrived_at + j].astype(jnp.float32)
                outgo[s][at + i] = total.astype(jnp.bfloat16)
                return carry

            def keep(i, carry):
                j = mine * half + i
                acc[s][base[s] + j] += arrived[s][arrived_at + j].astype(jnp.float32)
                return carry

            lax.fori_loop(0, half, pack, 0)
            copies[s] = place.send(
                outgo[s].at[pl.ds(at, half)], income[s].at[pl.ds(at, half)], k, sems, step, s
            )
            lax.fori_loop(0, half, keep, 0)
            base[s] = base[s] + mine * half
        arrived, arrived_at, at = income, at, at + half
    results = []
    for s in range(2):
        copies[s].wait()
        results.append(acc[s][base[s]] + arrived[s][arrived_at].astype(jnp.float32))
    return results


def gather_product(place, g_ref, held, total, sems):
    n, depth, width = place.n, held[0].shape[1], held[0].shape[2]

    def multiply(s, start, count):
        order = place.orders[s]

        def body(i, carry):
            slot = start + i
            block = sum(
                lax.rem(lax.div(slot, 2 ** (place.steps - 1 - i)), 2) * 2**k
                for i, k in enumerate(order)
            )
            columns = pl.ds(pl.multiple_of(block * width, 128), width)
            total[s * depth : (s + 1) * depth, :] += lax.dot_general(
                held[s][slot],
                g_ref[:, columns],
                (((1,), (1,)), ((), ())),
                preferred_element_type=jnp.float32,
            )
            return carry

        lax.fori_loop(0, count, body, 0)

    total[...] = jnp.zeros_like(total)
    base = [place.slot(place.me, place.orders[s]) for s in range(2)]
    fresh = list(base)
    count = 1
    for step in reversed(range(place.steps)):
        half = n >> (step + 1)
        copies = []
        for s in range(2):
            region = held[s].at[pl.ds(base[s], half)]
            copies.append(place.send(region, region, place.orders[s][step], sems, step, s))
        for s in range(2):
            multiply(s, fresh[s], count)
        for s in range(2):
            copies[s].wait()
            mine = place.bit(place.orders[s][step])
            fresh[s] = base[s] + (1 - 2 * mine) * half
            base[s] = base[s] - mine * half
        count = half
    for s in range(2):
        multiply(s, fresh[s], count)


def gram_total(place, y, sums, income, sems):
    sums[0] = lax.dot_general(
        y, y, (((1,), (1,)), ((), ())),
        precision=lax.Precision.HIGHEST, preferred_element_type=jnp.float32,
    )
    for k in range(place.steps):
        place.send(sums.at[k], income.at[k], k, sems, k).wait()
        sums[k + 1] = sums[k] + income[k]
    return sums[place.steps]


def finish(place, weights_ref, y_ref, gram_ref, total, sums, income, sems):
    y_ref[...] = total[...] * weights_ref[...]
    gram_ref[...] = gram_total(place, y_ref[...], sums, income, sems)


def first_kernel(n, g_ref, omega_ref, weights_ref, y_ref, gram_ref, h0, h1, total, sums, gin, ag_sems, gram_sems):
    place = Place(n)
    depth = h0.shape[1]
    for s, held in enumerate((h0, h1)):
        held[place.slot(place.me, place.orders[s])] = omega_ref[s * depth : (s + 1) * depth]
    place.greet()
    gather_product(place, g_ref, (h0, h1), total, ag_sems)
    finish(place, weights_ref, y_ref, gram_ref, total, sums, gin, gram_sems)


def second_kernel(n, scale, g_ref, w_ref, weights_ref, y_ref, gram_ref,
                  a0, a1, f0, f1, o0, o1, i0, i1, rs_sems,
                  h0, h1, total, sums, gin, ag_sems, gram_sems):
    place = Place(n)
    place.greet()
    results = reduce_scatter(place, g_ref, w_ref, (a0, a1), (f0, f1), (o0, o1), (i0, i1), rs_sems)
    for s, held in enumerate((h0, h1)):
        held[place.slot(place.me, place.orders[s])] = (results[s] * scale).astype(jnp.bfloat16)
    gather_product(place, g_ref, (h0, h1), total, ag_sems)
    finish(place, weights_ref, y_ref, gram_ref, total, sums, gin, gram_sems)


def last_kernel(n, scale, g_ref, w_ref, out_ref, a0, a1, f0, f1, o0, o1, i0, i1, rs_sems):
    place = Place(n)
    depth = a0.shape[1]
    place.greet()
    results = reduce_scatter(place, g_ref, w_ref, (a0, a1), (f0, f1), (o0, o1), (i0, i1), rs_sems)
    for s in range(2):
        out_ref[s * depth : (s + 1) * depth] = results[s] * scale


def local(greens, track_id, sigma_inv, sketch):
    rows, params = greens.shape
    columns = sketch.shape[0]
    n = lax.axis_size("row")
    steps = n.bit_length() - 1
    width, depth = params // n, columns // 2
    total_rows = rows * n
    scale = 1.0 / float(total_rows) ** 0.5
    groups = jnp.arange(sigma_inv.shape[0], dtype=jnp.int32)
    onehot = (track_id[:, None] == groups[None, :]).astype(jnp.float32)
    weights = jnp.dot(onehot, sigma_inv, precision=lax.Precision.HIGHEST)[None, :]
    f32, bf16 = jnp.float32, jnp.bfloat16

    scatter_scratch = (
        [pltpu.VMEM((n, depth, width), f32)] * 2
        + [pltpu.VMEM((n // 2, depth, width), f32)] * 2
        + [pltpu.VMEM((n // 2, depth, width), bf16)] * 4
        + [pltpu.SemaphoreType.DMA((2, steps, 2))]
    )
    gather_scratch = [pltpu.VMEM((n, depth, width), bf16)] * 2 + [
        pltpu.VMEM((columns, rows), f32),
        pltpu.VMEM((steps + 1, columns, columns), f32),
        pltpu.VMEM((steps, columns, columns), f32),
        pltpu.SemaphoreType.DMA((2, steps, 2)),
        pltpu.SemaphoreType.DMA((2, steps)),
    ]
    vmem = pl.BlockSpec(memory_space=pltpu.VMEM)
    flops = 2 * rows * params * columns
    product_shapes = (
        jax.ShapeDtypeStruct((columns, rows), f32),
        jax.ShapeDtypeStruct((columns, columns), f32),
    )

    def call(kernel, number, shapes, scratch, *operands):
        return pl.pallas_call(
            kernel,
            out_shape=shapes,
            in_specs=[vmem] * len(operands),
            out_specs=jax.tree.map(lambda _: vmem, shapes),
            scratch_shapes=scratch,
            cost_estimate=pl.CostEstimate(
                flops=flops, bytes_accessed=2 * rows * params, transcendentals=0
            ),
            compiler_params=pltpu.CompilerParams(
                collective_id=number, has_side_effects=True, vmem_limit_bytes=VMEM_LIMIT
            ),
        )(*operands)

    def orthonormal(sketched, gram):
        factor = jnp.linalg.cholesky(gram / total_rows)
        return lax.linalg.triangular_solve(factor, sketched, left_side=True, lower=True)

    omega = smooth(sketch).astype(bf16).reshape(columns, width)
    first, gram = call(
        functools.partial(first_kernel, n), 0, product_shapes, gather_scratch, greens, omega, weights
    )
    weighted_one = (orthonormal(first, gram) * weights).astype(bf16)
    second, gram = call(
        functools.partial(second_kernel, n, scale), 1, product_shapes,
        scatter_scratch + gather_scratch, greens, weighted_one, weights,
    )
    basis = orthonormal(second, gram)
    weighted_two = (basis * weights).astype(bf16)
    projected = call(
        functools.partial(last_kernel, n, scale), 2,
        jax.ShapeDtypeStruct((columns, width), f32), scatter_scratch, greens, weighted_two,
    )
    coefficients = projected.reshape(sketch.shape).transpose(1, 2, 0)
    return (basis.T, coefficients)


def solution(mesh):
    in_specs = (P(("grp", "row"), None), P(("grp", "row")), P("grp"), P("grp", "row", None))
    out_specs = (P(("grp", "row"), None), P(("grp", "row"), None, None))
    return jax.shard_map(local, mesh=mesh, in_specs=in_specs, out_specs=out_specs, check_vma=False)
```

```python
import functools
import jax
import jax.numpy as jnp
from jax import lax
from jax.experimental import pallas as pl
from jax.experimental.pallas import tpu as pltpu
from jax.sharding import PartitionSpec as P

SWEEPS = 4
smoothing = 0.24
VMEM_LIMIT = 52 * 1024 * 1024


def smooth(sketch):
    length = sketch.shape[1]
    count = lax.axis_size("row")
    before, after = [], []
    for hop in range(1, -(-SWEEPS // length) + 1):
        take = min(length, SWEEPS - (hop - 1) * length)
        up = [(i, i + hop) for i in range(count - hop)]
        down = [(j, i) for i, j in up]
        before.insert(0, lax.ppermute(sketch[:, length - take :], "row", up))
        after.append(lax.ppermute(sketch[:, :take], "row", down))
    field = jnp.concatenate(before + [sketch] + after, axis=1)
    first_row = lax.axis_index("row") * length - SWEEPS
    for sweep in range(1, SWEEPS + 1):
        padded = jnp.pad(field, ((0, 0), (0, 0), (1, 1)))
        centre = field[:, 1:-1]
        beside_all = (
            padded[:, 2:, 1:-1] + padded[:, :-2, 1:-1] + padded[:, 1:-1, 2:] + padded[:, 1:-1, :-2]
        )
        field = centre + smoothing * (beside_all - 4.0 * centre)
        if sweep < SWEEPS:
            rows = first_row + sweep + jnp.arange(field.shape[1], dtype=jnp.int32)
            inside = (rows >= 0) & (rows < length * count)
            field = jnp.where(inside[None, :, None], field, 0.0)
    return field


class Place:
    def __init__(self, n):
        self.n = n
        self.steps = n.bit_length() - 1
        self.me = lax.axis_index("row")
        rest = list(range(1, self.steps))
        self.orders = ([0] + rest, [0] + rest[1:] + rest[:1])

    def bit(self, k, of=None):
        return lax.rem(lax.div(self.me if of is None else of, 2**k), 2)

    def partner(self, k):
        return {"row": self.me + 2**k * (1 - 2 * self.bit(k))}

    def slot(self, block, order):
        return sum(self.bit(k, block) * 2 ** (self.steps - 1 - i) for i, k in enumerate(order))

    def greet(self):
        barrier = pltpu.get_barrier_semaphore()
        for k in range(self.steps):
            pl.semaphore_signal(
                barrier, inc=1, device_id=self.partner(k), device_id_type=pl.DeviceIdType.MESH
            )
        pl.semaphore_wait(barrier, self.steps)

    def send(self, source, target, k, sems, *at):
        copy = pltpu.make_async_remote_copy(
            src_ref=source,
            dst_ref=target,
            send_sem=sems.at[(0, *at)],
            recv_sem=sems.at[(1, *at)],
            device_id=self.partner(k),
            device_id_type=pl.DeviceIdType.MESH,
        )
        copy.start()
        return copy


def fetch(g_hbm, g_ref, loads, width):
    def copy(block):
        columns = pl.ds(pl.multiple_of(block * width, 128), width)
        return pltpu.make_async_copy(g_hbm.at[:, columns], g_ref.at[:, columns], loads.at[block])

    return copy


def quarters(place):
    a, b = place.bit(1), place.bit(2)
    return ((1 - a, 1 - b), (1 - a, b), (a, 1 - b), (a, b))


def over_blocks(place, core, quarter, visit):
    first = core + 2 * quarter[0] + 4 * quarter[1]

    def body(j, carry):
        visit(8 * j + first)
        return carry

    lax.fori_loop(0, place.n // 8, body, 0)


def start_loads(place, load):
    own = place.bit(0)
    for core in (1 - own, own):
        for quarter in quarters(place):
            over_blocks(place, core, quarter, lambda block: load(block).start())


def reduce_scatter(place, load, g_ref, w_ref, acc, wide, outgo, income, sems):
    n, depth = place.n, acc[0].shape[1]
    width = acc[0].shape[2]
    own = place.bit(0)
    parts = quarters(place)
    fourth = n // 4

    def produce(core, quarter):
        def visit(block):
            load(block).wait()
            columns = pl.ds(pl.multiple_of(block * width, 128), width)
            part = jnp.dot(w_ref[...], g_ref[:, columns], preferred_element_type=jnp.float32)
            for s in range(2):
                acc[s][place.slot(block, place.orders[s])] = part[s * depth : (s + 1) * depth]

        over_blocks(place, core, quarter, visit)

    def across(s, piece):
        mine = place.bit(place.orders[s][1])
        at = (1 - mine if piece == 0 else mine) * fourth
        return place.send(
            acc[s].at[pl.ds((1 - own) * (n // 2) + at, fourth)],
            wide[s].at[pl.ds(at, fourth)], 0, sems, place.steps if piece else 0, s,
        )

    pieces = [[None, None], [None, None]]
    produce(1 - own, parts[0])
    produce(1 - own, parts[1])
    pieces[0][0] = across(0, 0)
    produce(1 - own, parts[2])
    pieces[1][0] = across(1, 0)
    produce(1 - own, parts[3])
    pieces[0][1] = across(0, 1)
    pieces[1][1] = across(1, 1)
    produce(own, parts[0])
    produce(own, parts[1])

    base = [own * (n // 2), own * (n // 2)]
    copies = [None, None]
    arrived, arrived_at, at = wide, 0, 0
    for step in range(1, place.steps):
        half = n >> (step + 1)

        def add(s, offset, target, target_at):
            def body(i, carry):
                j = offset + i
                sum_ = acc[s][base[s] + j] + arrived[s][arrived_at + j].astype(jnp.float32)
                target[s][target_at + i] = sum_.astype(target[s].dtype)
                return carry

            lax.fori_loop(0, half, body, 0)

        def out(s):
            (pieces[s][0] if step == 1 else copies[s]).wait()
            k = place.orders[s][step]
            add(s, (1 - place.bit(k)) * half, outgo, at)
            copies[s] = place.send(
                outgo[s].at[pl.ds(at, half)], income[s].at[pl.ds(at, half)], k, sems, step, s
            )

        def keep(s):
            mine = place.bit(place.orders[s][step])
            if step == 1:
                pieces[s][1].wait()
            add(s, mine * half, acc, base[s] + mine * half)
            base[s] = base[s] + mine * half

        if step == 1:
            out(0)
            produce(own, parts[2])
            out(1)
            produce(own, parts[3])
            keep(0)
            keep(1)
        else:
            for s in range(2):
                out(s)
                keep(s)
        arrived, arrived_at, at = income, at, at + half
    results = []
    for s in range(2):
        copies[s].wait()
        results.append(acc[s][base[s]] + arrived[s][arrived_at].astype(jnp.float32))
    return results


def gather_product(place, g_ref, held, total, sems, ready=None):
    n, depth, width = place.n, held[0].shape[1], held[0].shape[2]
    over = (1 - 2 * place.bit(0)) * (n // 2)

    def multiply(s, start, count):
        order = place.orders[s]

        def body(i, carry):
            slot = start + i
            block = sum(
                lax.rem(lax.div(slot, 2 ** (place.steps - 1 - i)), 2) * 2**k
                for i, k in enumerate(order)
            )
            columns = pl.ds(pl.multiple_of(block * width, 128), width)
            total[s * depth : (s + 1) * depth, :] += lax.dot_general(
                held[s][slot],
                g_ref[:, columns],
                (((1,), (1,)), ((), ())),
                preferred_element_type=jnp.float32,
            )
            return carry

        lax.fori_loop(0, count, body, 0)

    def forward(s, step):
        region = held[s].at[pl.ds(fresh[s], count)]
        return place.send(region, region, 0, sems, place.steps + step, s)

    total[...] = jnp.zeros_like(total)
    base = [place.slot(place.me, place.orders[s]) for s in range(2)]
    fresh = list(base)
    count = 1
    for step in reversed(range(1, place.steps)):
        half = n >> (step + 1)
        copies = []
        for s in range(2):
            region = held[s].at[pl.ds(base[s], half)]
            copies.append(place.send(region, region, place.orders[s][step], sems, step, s))
        across = [forward(s, step) for s in range(2)]
        if ready is not None:
            ready()
            ready = None
        for s in range(2):
            multiply(s, fresh[s], count)
        for s in range(2):
            across[s].wait()
            multiply(s, fresh[s] + over, count)
        for s in range(2):
            copies[s].wait()
            mine = place.bit(place.orders[s][step])
            fresh[s] = base[s] + (1 - 2 * mine) * half
            base[s] = base[s] - mine * half
        count = half
    across = [forward(s, 0) for s in range(2)]
    for s in range(2):
        multiply(s, fresh[s], count)
    for s in range(2):
        across[s].wait()
        multiply(s, fresh[s] + over, count)


def gram_total(place, y, sums, income, sems):
    sums[0] = lax.dot_general(
        y, y, (((1,), (1,)), ((), ())),
        precision=lax.Precision.HIGHEST, preferred_element_type=jnp.float32,
    )
    for k in range(place.steps):
        place.send(sums.at[k], income.at[k], k, sems, k).wait()
        sums[k + 1] = sums[k] + income[k]
    return sums[place.steps]


def finish(place, weights_ref, y_ref, gram_ref, total, sums, income, sems):
    y_ref[...] = total[...] * weights_ref[...]
    gram_ref[...] = gram_total(place, y_ref[...], sums, income, sems)


def first_kernel(n, g_hbm, omega_ref, weights_ref, y_ref, gram_ref, g_ref, loads, h0, h1, total, sums, gin, ag_sems, gram_sems):
    place = Place(n)
    depth, width = h0.shape[1:]
    load = fetch(g_hbm, g_ref, loads, width)
    start_loads(place, load)

    def ready():
        def body(block, carry):
            load(block).wait()
            return carry

        lax.fori_loop(0, n, body, 0)

    for s, held in enumerate((h0, h1)):
        held[place.slot(place.me, place.orders[s])] = omega_ref[s * depth : (s + 1) * depth]
    place.greet()
    gather_product(place, g_ref, (h0, h1), total, ag_sems, ready)
    finish(place, weights_ref, y_ref, gram_ref, total, sums, gin, gram_sems)


def second_kernel(n, scale, g_hbm, w_ref, weights_ref, y_ref, gram_ref, g_ref, loads,
                  a0, a1, f0, f1, o0, o1, i0, i1, rs_sems,
                  h0, h1, total, sums, gin, ag_sems, gram_sems):
    place = Place(n)
    load = fetch(g_hbm, g_ref, loads, a0.shape[2])
    start_loads(place, load)
    place.greet()
    results = reduce_scatter(place, load, g_ref, w_ref, (a0, a1), (f0, f1), (o0, o1), (i0, i1), rs_sems)
    for s, held in enumerate((h0, h1)):
        held[place.slot(place.me, place.orders[s])] = (results[s] * scale).astype(jnp.bfloat16)
    gather_product(place, g_ref, (h0, h1), total, ag_sems)
    finish(place, weights_ref, y_ref, gram_ref, total, sums, gin, gram_sems)


def last_kernel(n, scale, g_hbm, w_ref, out_ref, g_ref, loads, a0, a1, f0, f1, o0, o1, i0, i1, rs_sems):
    place = Place(n)
    depth, width = a0.shape[1:]
    load = fetch(g_hbm, g_ref, loads, width)
    start_loads(place, load)
    place.greet()
    results = reduce_scatter(place, load, g_ref, w_ref, (a0, a1), (f0, f1), (o0, o1), (i0, i1), rs_sems)
    for s in range(2):
        out_ref[s * depth : (s + 1) * depth] = results[s] * scale


def local(greens, track_id, sigma_inv, sketch):
    rows, params = greens.shape
    columns = sketch.shape[0]
    n = lax.axis_size("row")
    steps = n.bit_length() - 1
    width, depth = params // n, columns // 2
    total_rows = rows * n
    scale = 1.0 / float(total_rows) ** 0.5
    groups = jnp.arange(sigma_inv.shape[0], dtype=jnp.int32)
    onehot = (track_id[:, None] == groups[None, :]).astype(jnp.float32)
    weights = jnp.dot(onehot, sigma_inv, precision=lax.Precision.HIGHEST)[None, :]
    f32, bf16 = jnp.float32, jnp.bfloat16

    scatter_scratch = (
        [pltpu.VMEM((n, depth, width), f32)] * 2
        + [pltpu.VMEM((n // 2, depth, width), f32)] * 2
        + [pltpu.VMEM((n // 2, depth, width), bf16)] * 4
        + [pltpu.SemaphoreType.DMA((2, steps + 1, 2))]
    )
    gather_scratch = [pltpu.VMEM((n, depth, width), bf16)] * 2 + [
        pltpu.VMEM((columns, rows), f32),
        pltpu.VMEM((steps + 1, columns, columns), f32),
        pltpu.VMEM((steps, columns, columns), f32),
        pltpu.SemaphoreType.DMA((2, 2 * steps, 2)),
        pltpu.SemaphoreType.DMA((2, steps)),
    ]
    vmem = pl.BlockSpec(memory_space=pltpu.VMEM)
    flops = 2 * rows * params * columns
    product_shapes = (
        jax.ShapeDtypeStruct((columns, rows), f32),
        jax.ShapeDtypeStruct((columns, columns), f32),
    )

    def call(kernel, number, shapes, scratch, *operands):
        return pl.pallas_call(
            kernel,
            out_shape=shapes,
            in_specs=[pl.BlockSpec(memory_space=pl.ANY)] + [vmem] * (len(operands) - 1),
            out_specs=jax.tree.map(lambda _: vmem, shapes),
            scratch_shapes=[pltpu.VMEM((rows, params), bf16), pltpu.SemaphoreType.DMA((n,))] + scratch,
            cost_estimate=pl.CostEstimate(
                flops=flops, bytes_accessed=2 * rows * params, transcendentals=0
            ),
            compiler_params=pltpu.CompilerParams(
                collective_id=number, has_side_effects=True, vmem_limit_bytes=VMEM_LIMIT
            ),
        )(*operands)

    def orthonormal(sketched, gram):
        factor = jnp.linalg.cholesky(gram / total_rows)
        return lax.linalg.triangular_solve(factor, sketched, left_side=True, lower=True)

    omega = smooth(sketch).astype(bf16).reshape(columns, width)
    first, gram = call(
        functools.partial(first_kernel, n), 0, product_shapes, gather_scratch, greens, omega, weights
    )
    weighted_one = (orthonormal(first, gram) * weights).astype(bf16)
    second, gram = call(
        functools.partial(second_kernel, n, scale), 1, product_shapes,
        scatter_scratch + gather_scratch, greens, weighted_one, weights,
    )
    basis = orthonormal(second, gram)
    weighted_two = (basis * weights).astype(bf16)
    projected = call(
        functools.partial(last_kernel, n, scale), 2,
        jax.ShapeDtypeStruct((columns, width), f32), scatter_scratch, greens, weighted_two,
    )
    coefficients = projected.reshape(sketch.shape).transpose(1, 2, 0)
    return (basis.T, coefficients)


def solution(mesh):
    in_specs = (P(("grp", "row"), None), P(("grp", "row")), P("grp"), P("grp", "row", None))
    out_specs = (P(("grp", "row"), None), P(("grp", "row"), None, None))
    return jax.shard_map(local, mesh=mesh, in_specs=in_specs, out_specs=out_specs, check_vma=False)
```

```python
import functools
import jax
import jax.numpy as jnp
from jax import lax
from jax.experimental import pallas as pl
from jax.experimental.pallas import tpu as pltpu
from jax.sharding import PartitionSpec as P

SWEEPS = 4
smoothing = 0.24
VMEM_LIMIT = 52 * 1024 * 1024


def smooth(sketch):
    length = sketch.shape[1]
    count = lax.axis_size("row")
    before, after = [], []
    for hop in range(1, -(-SWEEPS // length) + 1):
        take = min(length, SWEEPS - (hop - 1) * length)
        up = [(i, i + hop) for i in range(count - hop)]
        down = [(j, i) for i, j in up]
        before.insert(0, lax.ppermute(sketch[:, length - take :], "row", up))
        after.append(lax.ppermute(sketch[:, :take], "row", down))
    field = jnp.concatenate(before + [sketch] + after, axis=1)
    first_row = lax.axis_index("row") * length - SWEEPS
    for sweep in range(1, SWEEPS + 1):
        padded = jnp.pad(field, ((0, 0), (0, 0), (1, 1)))
        centre = field[:, 1:-1]
        beside_all = (
            padded[:, 2:, 1:-1] + padded[:, :-2, 1:-1] + padded[:, 1:-1, 2:] + padded[:, 1:-1, :-2]
        )
        field = centre + smoothing * (beside_all - 4.0 * centre)
        if sweep < SWEEPS:
            rows = first_row + sweep + jnp.arange(field.shape[1], dtype=jnp.int32)
            inside = (rows >= 0) & (rows < length * count)
            field = jnp.where(inside[None, :, None], field, 0.0)
    return field


class Place:
    def __init__(self, n):
        self.n = n
        self.steps = n.bit_length() - 1
        self.me = lax.axis_index("row")
        rest = list(range(1, self.steps))
        self.orders = ([0] + rest, [0] + rest[1:] + rest[:1])

    def bit(self, k, of=None):
        return lax.rem(lax.div(self.me if of is None else of, 2**k), 2)

    def partner(self, k):
        return {"row": self.me + 2**k * (1 - 2 * self.bit(k))}

    def slot(self, block, order):
        return sum(self.bit(k, block) * 2 ** (self.steps - 1 - i) for i, k in enumerate(order))

    def greet(self):
        barrier = pltpu.get_barrier_semaphore()
        for k in range(self.steps):
            pl.semaphore_signal(
                barrier, inc=1, device_id=self.partner(k), device_id_type=pl.DeviceIdType.MESH
            )
        pl.semaphore_wait(barrier, self.steps)

    def send(self, source, target, k, sems, *at):
        copy = pltpu.make_async_remote_copy(
            src_ref=source,
            dst_ref=target,
            send_sem=sems.at[(0, *at)],
            recv_sem=sems.at[(1, *at)],
            device_id=self.partner(k),
            device_id_type=pl.DeviceIdType.MESH,
        )
        copy.start()
        return copy


def fetch(g_hbm, g_ref, loads, width):
    def copy(block):
        columns = pl.ds(pl.multiple_of(block * width, 128), width)
        return pltpu.make_async_copy(g_hbm.at[:, columns], g_ref.at[:, columns], loads.at[block])

    return copy


def quarters(place):
    a, b = place.bit(1), place.bit(2)
    return ((1 - a, 1 - b), (1 - a, b), (a, 1 - b), (a, b))


def over_blocks(place, core, quarter, visit):
    first = core + 2 * quarter[0] + 4 * quarter[1]

    def body(j, carry):
        visit(8 * j + first)
        return carry

    lax.fori_loop(0, place.n // 8, body, 0)


def start_loads(place, load):
    own = place.bit(0)
    for core in (1 - own, own):
        for quarter in quarters(place):
            over_blocks(place, core, quarter, lambda block: load(block).start())


def reduce_scatter(place, load, g_ref, w_ref, acc, wide, outgo, income, sems):
    n, depth = place.n, acc[0].shape[1]
    width = acc[0].shape[2]
    own = place.bit(0)
    parts = quarters(place)
    fourth = n // 4

    def produce(core, quarter):
        def visit(block):
            load(block).wait()
            columns = pl.ds(pl.multiple_of(block * width, 128), width)
            part = jnp.dot(w_ref[...], g_ref[:, columns], preferred_element_type=jnp.float32)
            for s in range(2):
                acc[s][place.slot(block, place.orders[s])] = part[s * depth : (s + 1) * depth]

        over_blocks(place, core, quarter, visit)

    def across(s, piece):
        mine = place.bit(place.orders[s][1])
        at = (1 - mine if piece == 0 else mine) * fourth
        return place.send(
            acc[s].at[pl.ds((1 - own) * (n // 2) + at, fourth)],
            wide[s].at[pl.ds(at, fourth)], 0, sems, place.steps if piece else 0, s,
        )

    pieces = [[None, None], [None, None]]
    produce(1 - own, parts[0])
    produce(1 - own, parts[1])
    pieces[0][0] = across(0, 0)
    produce(1 - own, parts[2])
    pieces[1][0] = across(1, 0)
    produce(1 - own, parts[3])
    pieces[0][1] = across(0, 1)
    pieces[1][1] = across(1, 1)
    produce(own, parts[0])
    produce(own, parts[1])

    base = [own * (n // 2), own * (n // 2)]
    copies = [None, None]
    arrived, arrived_at, at = wide, 0, 0
    for step in range(1, place.steps):
        half = n >> (step + 1)

        def add(s, offset, target, target_at):
            def body(i, carry):
                j = offset + i
                sum_ = acc[s][base[s] + j] + arrived[s][arrived_at + j].astype(jnp.float32)
                target[s][target_at + i] = sum_.astype(target[s].dtype)
                return carry

            lax.fori_loop(0, half, body, 0)

        def out(s):
            (pieces[s][0] if step == 1 else copies[s]).wait()
            k = place.orders[s][step]
            add(s, (1 - place.bit(k)) * half, outgo, at)
            copies[s] = place.send(
                outgo[s].at[pl.ds(at, half)], income[s].at[pl.ds(at, half)], k, sems, step, s
            )

        def keep(s):
            mine = place.bit(place.orders[s][step])
            if step == 1:
                pieces[s][1].wait()
            add(s, mine * half, acc, base[s] + mine * half)
            base[s] = base[s] + mine * half

        if step == 1:
            out(0)
            produce(own, parts[2])
            out(1)
            produce(own, parts[3])
            keep(0)
            keep(1)
        else:
            for s in range(2):
                out(s)
                keep(s)
        arrived, arrived_at, at = income, at, at + half
    results = []
    for s in range(2):
        copies[s].wait()
        results.append(acc[s][base[s]] + arrived[s][arrived_at].astype(jnp.float32))
    return results


def gather_product(place, g_ref, held, total, sems, ready=None):
    n, depth, width = place.n, held[0].shape[1], held[0].shape[2]
    over = (1 - 2 * place.bit(0)) * (n // 2)

    def multiply(s, start, count):
        order = place.orders[s]

        def body(i, carry):
            slot = start + i
            block = sum(
                lax.rem(lax.div(slot, 2 ** (place.steps - 1 - i)), 2) * 2**k
                for i, k in enumerate(order)
            )
            columns = pl.ds(pl.multiple_of(block * width, 128), width)
            total[s * depth : (s + 1) * depth, :] += lax.dot_general(
                held[s][slot],
                g_ref[:, columns],
                (((1,), (1,)), ((), ())),
                preferred_element_type=jnp.float32,
            )
            return carry

        lax.fori_loop(0, count, body, 0)

    def forward(s, step):
        region = held[s].at[pl.ds(fresh[s], count)]
        return place.send(region, region, 0, sems, place.steps + step, s)

    total[...] = jnp.zeros_like(total)
    base = [place.slot(place.me, place.orders[s]) for s in range(2)]
    fresh = list(base)
    count = 1
    for step in reversed(range(1, place.steps)):
        half = n >> (step + 1)
        copies = []
        for s in range(2):
            region = held[s].at[pl.ds(base[s], half)]
            copies.append(place.send(region, region, place.orders[s][step], sems, step, s))
        across = [forward(s, step) for s in range(2)]
        if ready is not None:
            ready()
            ready = None
        for s in range(2):
            multiply(s, fresh[s], count)
        for s in range(2):
            across[s].wait()
            multiply(s, fresh[s] + over, count)
        for s in range(2):
            copies[s].wait()
            mine = place.bit(place.orders[s][step])
            fresh[s] = base[s] + (1 - 2 * mine) * half
            base[s] = base[s] - mine * half
        count = half
    across = [forward(s, 0) for s in range(2)]
    for s in range(2):
        multiply(s, fresh[s], count)
    for s in range(2):
        across[s].wait()
        multiply(s, fresh[s] + over, count)


def gram_total(place, y, sums, income, sems):
    sums[0] = lax.dot_general(
        y, y, (((1,), (1,)), ((), ())),
        precision=lax.Precision.HIGHEST, preferred_element_type=jnp.float32,
    )
    for k in range(place.steps):
        place.send(sums.at[k], income.at[k], k, sems, k).wait()
        sums[k + 1] = sums[k] + income[k]
    return sums[place.steps]


def finish(place, weights_ref, y_ref, gram_ref, total, sums, income, sems):
    y_ref[...] = total[...] * weights_ref[...]
    gram_ref[...] = gram_total(place, y_ref[...], sums, income, sems)


def first_kernel(n, g_hbm, omega_ref, weights_ref, y_ref, gram_ref, g_ref, loads, h0, h1, total, sums, gin, ag_sems, gram_sems):
    place = Place(n)
    depth, width = h0.shape[1:]
    load = fetch(g_hbm, g_ref, loads, width)
    start_loads(place, load)

    def ready():
        def body(block, carry):
            load(block).wait()
            return carry

        lax.fori_loop(0, n, body, 0)

    for s, held in enumerate((h0, h1)):
        held[place.slot(place.me, place.orders[s])] = omega_ref[s * depth : (s + 1) * depth]
    place.greet()
    gather_product(place, g_ref, (h0, h1), total, ag_sems, ready)
    finish(place, weights_ref, y_ref, gram_ref, total, sums, gin, gram_sems)


def second_kernel(n, scale, g_hbm, w_ref, weights_ref, y_ref, gram_ref, g_ref, loads,
                  a0, a1, f0, f1, o0, o1, i0, i1, rs_sems,
                  h0, h1, total, sums, gin, ag_sems, gram_sems):
    place = Place(n)
    load = fetch(g_hbm, g_ref, loads, a0.shape[2])
    start_loads(place, load)
    place.greet()
    results = reduce_scatter(place, load, g_ref, w_ref, (a0, a1), (f0, f1), (o0, o1), (i0, i1), rs_sems)
    for s, held in enumerate((h0, h1)):
        held[place.slot(place.me, place.orders[s])] = (results[s] * scale).astype(jnp.bfloat16)
    gather_product(place, g_ref, (h0, h1), total, ag_sems)
    finish(place, weights_ref, y_ref, gram_ref, total, sums, gin, gram_sems)


def last_kernel(n, scale, g_hbm, w_ref, out_ref, g_ref, loads, a0, a1, f0, f1, o0, o1, i0, i1, rs_sems):
    place = Place(n)
    depth, width = a0.shape[1:]
    load = fetch(g_hbm, g_ref, loads, width)
    start_loads(place, load)
    place.greet()
    results = reduce_scatter(place, load, g_ref, w_ref, (a0, a1), (f0, f1), (o0, o1), (i0, i1), rs_sems)
    for s in range(2):
        out_ref[s * depth : (s + 1) * depth] = results[s] * scale


def orthonormal_kernel(total_rows, gram_ref, y_ref, weights_ref, basis_ref, weighted_ref, inverse):
    size = gram_ref.shape[0]
    lane = lax.broadcasted_iota(jnp.int32, (1, size), 1)
    below = lax.broadcasted_iota(jnp.int32, (8, 1), 0)
    groups = [gram_ref[i : i + 8] / total_rows for i in range(0, size, 8)]
    for k in range(size):
        own, place = k // 8, k % 8
        row = groups[own][place : place + 1]
        pivot = row[:, k : k + 1]
        row = jnp.where(lane == k, 1.0, row)
        inverse[k : k + 1] = jnp.where(lane <= k, row, 0.0) * lax.rsqrt(pivot)
        row = row / pivot
        for g in range(own, size // 8):
            column = groups[g][:, k : k + 1]
            cleared = jnp.where(lane == k, 0.0, groups[g])
            if g == own:
                groups[g] = jnp.where(below > place, cleared - column * row, groups[g])
            else:
                groups[g] = cleared - column * row
    basis = jnp.dot(
        inverse[...], y_ref[...],
        precision=lax.Precision.HIGHEST, preferred_element_type=jnp.float32,
    )
    basis_ref[...] = basis
    weighted_ref[...] = (basis * weights_ref[...]).astype(jnp.bfloat16)


def local(greens, track_id, sigma_inv, sketch):
    rows, params = greens.shape
    columns = sketch.shape[0]
    n = lax.axis_size("row")
    steps = n.bit_length() - 1
    width, depth = params // n, columns // 2
    total_rows = rows * n
    scale = 1.0 / float(total_rows) ** 0.5
    groups = jnp.arange(sigma_inv.shape[0], dtype=jnp.int32)
    onehot = (track_id[:, None] == groups[None, :]).astype(jnp.float32)
    weights = jnp.dot(onehot, sigma_inv, precision=lax.Precision.HIGHEST)[None, :]
    f32, bf16 = jnp.float32, jnp.bfloat16

    scatter_scratch = (
        [pltpu.VMEM((n, depth, width), f32)] * 2
        + [pltpu.VMEM((n // 2, depth, width), f32)] * 2
        + [pltpu.VMEM((n // 2, depth, width), bf16)] * 4
        + [pltpu.SemaphoreType.DMA((2, steps + 1, 2))]
    )
    gather_scratch = [pltpu.VMEM((n, depth, width), bf16)] * 2 + [
        pltpu.VMEM((columns, rows), f32),
        pltpu.VMEM((steps + 1, columns, columns), f32),
        pltpu.VMEM((steps, columns, columns), f32),
        pltpu.SemaphoreType.DMA((2, 2 * steps, 2)),
        pltpu.SemaphoreType.DMA((2, steps)),
    ]
    vmem = pl.BlockSpec(memory_space=pltpu.VMEM)
    flops = 2 * rows * params * columns
    product_shapes = (
        jax.ShapeDtypeStruct((columns, rows), f32),
        jax.ShapeDtypeStruct((columns, columns), f32),
    )

    def call(kernel, number, shapes, scratch, *operands):
        return pl.pallas_call(
            kernel,
            out_shape=shapes,
            in_specs=[pl.BlockSpec(memory_space=pl.ANY)] + [vmem] * (len(operands) - 1),
            out_specs=jax.tree.map(lambda _: vmem, shapes),
            scratch_shapes=[pltpu.VMEM((rows, params), bf16), pltpu.SemaphoreType.DMA((n,))] + scratch,
            cost_estimate=pl.CostEstimate(
                flops=flops, bytes_accessed=2 * rows * params, transcendentals=0
            ),
            compiler_params=pltpu.CompilerParams(
                collective_id=number, has_side_effects=True, vmem_limit_bytes=VMEM_LIMIT
            ),
        )(*operands)

    def orthonormal(sketched, gram):
        return pl.pallas_call(
            functools.partial(orthonormal_kernel, float(total_rows)),
            out_shape=(
                jax.ShapeDtypeStruct((columns, rows), f32),
                jax.ShapeDtypeStruct((columns, rows), bf16),
            ),
            in_specs=[vmem] * 3,
            out_specs=(vmem, vmem),
            scratch_shapes=[pltpu.VMEM((columns, columns), f32)],
        )(gram, sketched, weights)

    omega = smooth(sketch).astype(bf16).reshape(columns, width)
    first, gram = call(
        functools.partial(first_kernel, n), 0, product_shapes, gather_scratch, greens, omega, weights
    )
    _, weighted_one = orthonormal(first, gram)
    second, gram = call(
        functools.partial(second_kernel, n, scale), 1, product_shapes,
        scatter_scratch + gather_scratch, greens, weighted_one, weights,
    )
    basis, weighted_two = orthonormal(second, gram)
    projected = call(
        functools.partial(last_kernel, n, scale), 2,
        jax.ShapeDtypeStruct((columns, width), f32), scatter_scratch, greens, weighted_two,
    )
    coefficients = projected.reshape(sketch.shape).transpose(1, 2, 0)
    return (basis.T, coefficients)


def solution(mesh):
    in_specs = (P(("grp", "row"), None), P(("grp", "row")), P("grp"), P("grp", "row", None))
    out_specs = (P(("grp", "row"), None), P(("grp", "row"), None, None))
    return jax.shard_map(local, mesh=mesh, in_specs=in_specs, out_specs=out_specs, check_vma=False)
```

```python
import functools
import jax
import jax.numpy as jnp
from jax import lax
from jax.experimental import pallas as pl
from jax.experimental.pallas import tpu as pltpu
from jax.sharding import PartitionSpec as P

SWEEPS = 4
smoothing = 0.24
VMEM_LIMIT = 52 * 1024 * 1024


def smooth(sketch):
    length = sketch.shape[1]
    count = lax.axis_size("row")
    before, after = [], []
    for hop in range(1, -(-SWEEPS // length) + 1):
        take = min(length, SWEEPS - (hop - 1) * length)
        up = [(i, i + hop) for i in range(count - hop)]
        down = [(j, i) for i, j in up]
        before.insert(0, lax.ppermute(sketch[:, length - take :], "row", up))
        after.append(lax.ppermute(sketch[:, :take], "row", down))
    field = jnp.concatenate(before + [sketch] + after, axis=1)
    first_row = lax.axis_index("row") * length - SWEEPS
    for sweep in range(1, SWEEPS + 1):
        padded = jnp.pad(field, ((0, 0), (0, 0), (1, 1)))
        centre = field[:, 1:-1]
        beside_all = (
            padded[:, 2:, 1:-1] + padded[:, :-2, 1:-1] + padded[:, 1:-1, 2:] + padded[:, 1:-1, :-2]
        )
        field = centre + smoothing * (beside_all - 4.0 * centre)
        if sweep < SWEEPS:
            rows = first_row + sweep + jnp.arange(field.shape[1], dtype=jnp.int32)
            inside = (rows >= 0) & (rows < length * count)
            field = jnp.where(inside[None, :, None], field, 0.0)
    return field


class Place:
    def __init__(self, n):
        self.n = n
        self.steps = n.bit_length() - 1
        self.me = lax.axis_index("row")
        rest = list(range(1, self.steps))
        self.orders = ([0] + rest, [0] + rest[1:] + rest[:1])

    def bit(self, k, of=None):
        return lax.rem(lax.div(self.me if of is None else of, 2**k), 2)

    def partner(self, k):
        return {"row": self.me + 2**k * (1 - 2 * self.bit(k))}

    def slot(self, block, order):
        return sum(self.bit(k, block) * 2 ** (self.steps - 1 - i) for i, k in enumerate(order))

    def greet(self):
        barrier = pltpu.get_barrier_semaphore()
        for k in range(self.steps):
            pl.semaphore_signal(
                barrier, inc=1, device_id=self.partner(k), device_id_type=pl.DeviceIdType.MESH
            )
        pl.semaphore_wait(barrier, self.steps)

    def send(self, source, target, k, sems, *at):
        copy = pltpu.make_async_remote_copy(
            src_ref=source,
            dst_ref=target,
            send_sem=sems.at[(0, *at)],
            recv_sem=sems.at[(1, *at)],
            device_id=self.partner(k),
            device_id_type=pl.DeviceIdType.MESH,
        )
        copy.start()
        return copy


def fetch(g_hbm, g_ref, loads, width):
    def copy(block):
        columns = pl.ds(pl.multiple_of(block * width, 128), width)
        return pltpu.make_async_copy(g_hbm.at[:, columns], g_ref.at[:, columns], loads.at[block])

    return copy


def quarters(place):
    a, b = place.bit(1), place.bit(2)
    return ((1 - a, 1 - b), (1 - a, b), (a, 1 - b), (a, b))


def over_blocks(place, core, quarter, visit):
    first = core + 2 * quarter[0] + 4 * quarter[1]

    def body(j, carry):
        visit(8 * j + first)
        return carry

    lax.fori_loop(0, place.n // 8, body, 0)


def start_loads(place, load):
    own = place.bit(0)
    for core in (1 - own, own):
        for quarter in quarters(place):
            over_blocks(place, core, quarter, lambda block: load(block).start())


def reduce_scatter(place, load, g_ref, w_ref, acc, cross, wide, outgo, income, sems):
    n, depth = place.n, acc[0].shape[1]
    width = acc[0].shape[2]
    own = place.bit(0)
    parts = quarters(place)
    fourth = n // 4

    def produce(core, quarter, target, skip):
        def visit(block):
            load(block).wait()
            columns = pl.ds(pl.multiple_of(block * width, 128), width)
            part = jnp.dot(w_ref[...], g_ref[:, columns], preferred_element_type=jnp.float32)
            for s in range(2):
                target[s][place.slot(block, place.orders[s]) - skip] = part[
                    s * depth : (s + 1) * depth
                ].astype(target[s].dtype)

        over_blocks(place, core, quarter, visit)

    def across(s, piece):
        mine = place.bit(place.orders[s][1])
        at = (1 - mine if piece == 0 else mine) * fourth
        return place.send(
            cross[s].at[pl.ds(at, fourth)],
            wide[s].at[pl.ds(at, fourth)], 0, sems, place.steps if piece else 0, s,
        )

    pieces = [[None, None], [None, None]]
    produce(1 - own, parts[0], cross, (1 - own) * (n // 2))
    produce(1 - own, parts[1], cross, (1 - own) * (n // 2))
    pieces[0][0] = across(0, 0)
    produce(1 - own, parts[2], cross, (1 - own) * (n // 2))
    pieces[1][0] = across(1, 0)
    produce(1 - own, parts[3], cross, (1 - own) * (n // 2))
    pieces[0][1] = across(0, 1)
    pieces[1][1] = across(1, 1)
    produce(own, parts[0], acc, 0)
    produce(own, parts[1], acc, 0)

    base = [own * (n // 2), own * (n // 2)]
    copies = [None, None]
    arrived, arrived_at, at = wide, 0, 0
    for step in range(1, place.steps):
        half = n >> (step + 1)

        def add(s, offset, target, target_at):
            def body(i, carry):
                j = offset + i
                sum_ = acc[s][base[s] + j] + arrived[s][arrived_at + j].astype(jnp.float32)
                target[s][target_at + i] = sum_.astype(target[s].dtype)
                return carry

            lax.fori_loop(0, half, body, 0)

        def out(s):
            (pieces[s][0] if step == 1 else copies[s]).wait()
            k = place.orders[s][step]
            add(s, (1 - place.bit(k)) * half, outgo, at)
            copies[s] = place.send(
                outgo[s].at[pl.ds(at, half)], income[s].at[pl.ds(at, half)], k, sems, step, s
            )

        def keep(s):
            mine = place.bit(place.orders[s][step])
            if step == 1:
                pieces[s][1].wait()
            add(s, mine * half, acc, base[s] + mine * half)
            base[s] = base[s] + mine * half

        if step == 1:
            out(0)
            produce(own, parts[2], acc, 0)
            out(1)
            produce(own, parts[3], acc, 0)
            keep(0)
            keep(1)
        else:
            for s in range(2):
                out(s)
                keep(s)
        arrived, arrived_at, at = income, at, at + half
    results = []
    for s in range(2):
        copies[s].wait()
        results.append(acc[s][base[s]] + arrived[s][arrived_at].astype(jnp.float32))
    return results


def gather_product(place, g_ref, held, total, sems, ready=None):
    n, depth, width = place.n, held[0].shape[1], held[0].shape[2]
    over = (1 - 2 * place.bit(0)) * (n // 2)

    def multiply(s, start, count):
        order = place.orders[s]

        def body(i, carry):
            slot = start + i
            block = sum(
                lax.rem(lax.div(slot, 2 ** (place.steps - 1 - i)), 2) * 2**k
                for i, k in enumerate(order)
            )
            columns = pl.ds(pl.multiple_of(block * width, 128), width)
            total[s * depth : (s + 1) * depth, :] += lax.dot_general(
                held[s][slot],
                g_ref[:, columns],
                (((1,), (1,)), ((), ())),
                preferred_element_type=jnp.float32,
            )
            return carry

        lax.fori_loop(0, count, body, 0)

    def forward(s, step):
        region = held[s].at[pl.ds(fresh[s], count)]
        return place.send(region, region, 0, sems, place.steps + step, s)

    total[...] = jnp.zeros_like(total)
    base = [place.slot(place.me, place.orders[s]) for s in range(2)]
    fresh = list(base)
    count = 1
    for step in reversed(range(1, place.steps)):
        half = n >> (step + 1)
        copies = []
        for s in range(2):
            region = held[s].at[pl.ds(base[s], half)]
            copies.append(place.send(region, region, place.orders[s][step], sems, step, s))
        across = [forward(s, step) for s in range(2)]
        if ready is not None:
            ready()
            ready = None
        for s in range(2):
            multiply(s, fresh[s], count)
        for s in range(2):
            across[s].wait()
            multiply(s, fresh[s] + over, count)
        for s in range(2):
            copies[s].wait()
            mine = place.bit(place.orders[s][step])
            fresh[s] = base[s] + (1 - 2 * mine) * half
            base[s] = base[s] - mine * half
        count = half
    across = [forward(s, 0) for s in range(2)]
    for s in range(2):
        multiply(s, fresh[s], count)
    for s in range(2):
        across[s].wait()
        multiply(s, fresh[s] + over, count)


def gram_total(place, y, sums, income, sems):
    sums[0] = lax.dot_general(
        y, y, (((1,), (1,)), ((), ())),
        precision=lax.Precision.HIGHEST, preferred_element_type=jnp.float32,
    )
    for k in range(place.steps):
        place.send(sums.at[k], income.at[k], k, sems, k).wait()
        sums[k + 1] = sums[k] + income[k]
    return sums[place.steps]


def finish(place, weights_ref, y_ref, gram_ref, total, sums, income, sems):
    y_ref[...] = total[...] * weights_ref[...]
    gram_ref[...] = gram_total(place, y_ref[...], sums, income, sems)


def first_kernel(n, g_hbm, omega_ref, weights_ref, y_ref, gram_ref, g_ref, loads, h0, h1, total, sums, gin, ag_sems, gram_sems):
    place = Place(n)
    depth, width = h0.shape[1:]
    load = fetch(g_hbm, g_ref, loads, width)
    start_loads(place, load)

    def ready():
        def body(block, carry):
            load(block).wait()
            return carry

        lax.fori_loop(0, n, body, 0)

    for s, held in enumerate((h0, h1)):
        held[place.slot(place.me, place.orders[s])] = omega_ref[s * depth : (s + 1) * depth]
    place.greet()
    gather_product(place, g_ref, (h0, h1), total, ag_sems, ready)
    finish(place, weights_ref, y_ref, gram_ref, total, sums, gin, gram_sems)


def second_kernel(n, scale, g_hbm, w_ref, weights_ref, y_ref, gram_ref, g_ref, loads,
                  a0, a1, c0, c1, f0, f1, o0, o1, i0, i1, rs_sems,
                  h0, h1, total, sums, gin, ag_sems, gram_sems):
    place = Place(n)
    load = fetch(g_hbm, g_ref, loads, a0.shape[2])
    start_loads(place, load)
    place.greet()
    results = reduce_scatter(place, load, g_ref, w_ref, (a0, a1), (c0, c1), (f0, f1), (o0, o1), (i0, i1), rs_sems)
    for s, held in enumerate((h0, h1)):
        held[place.slot(place.me, place.orders[s])] = (results[s] * scale).astype(jnp.bfloat16)
    gather_product(place, g_ref, (h0, h1), total, ag_sems)
    finish(place, weights_ref, y_ref, gram_ref, total, sums, gin, gram_sems)


def last_kernel(n, scale, g_hbm, w_ref, out_ref, g_ref, loads, a0, a1, c0, c1, f0, f1, o0, o1, i0, i1, rs_sems):
    place = Place(n)
    depth, width = a0.shape[1:]
    load = fetch(g_hbm, g_ref, loads, width)
    start_loads(place, load)
    place.greet()
    results = reduce_scatter(place, load, g_ref, w_ref, (a0, a1), (c0, c1), (f0, f1), (o0, o1), (i0, i1), rs_sems)
    for s in range(2):
        out_ref[s * depth : (s + 1) * depth] = results[s] * scale


def orthonormal_kernel(total_rows, gram_ref, y_ref, weights_ref, basis_ref, weighted_ref, inverse):
    size = gram_ref.shape[0]
    lane = lax.broadcasted_iota(jnp.int32, (1, size), 1)
    below = lax.broadcasted_iota(jnp.int32, (8, 1), 0)
    groups = [gram_ref[i : i + 8] / total_rows for i in range(0, size, 8)]
    for k in range(size):
        own, place = k // 8, k % 8
        row = groups[own][place : place + 1]
        pivot = row[:, k : k + 1]
        row = jnp.where(lane == k, 1.0, row)
        inverse[k : k + 1] = jnp.where(lane <= k, row, 0.0) * lax.rsqrt(pivot)
        row = row / pivot
        for g in range(own, size // 8):
            column = groups[g][:, k : k + 1]
            cleared = jnp.where(lane == k, 0.0, groups[g])
            if g == own:
                groups[g] = jnp.where(below > place, cleared - column * row, groups[g])
            else:
                groups[g] = cleared - column * row
    basis = jnp.dot(
        inverse[...], y_ref[...],
        precision=lax.Precision.HIGHEST, preferred_element_type=jnp.float32,
    )
    basis_ref[...] = basis
    weighted_ref[...] = (basis * weights_ref[...]).astype(jnp.bfloat16)


def local(greens, track_id, sigma_inv, sketch):
    rows, params = greens.shape
    columns = sketch.shape[0]
    n = lax.axis_size("row")
    steps = n.bit_length() - 1
    width, depth = params // n, columns // 2
    total_rows = rows * n
    scale = 1.0 / float(total_rows) ** 0.5
    groups = jnp.arange(sigma_inv.shape[0], dtype=jnp.int32)
    onehot = (track_id[:, None] == groups[None, :]).astype(jnp.float32)
    weights = jnp.dot(onehot, sigma_inv, precision=lax.Precision.HIGHEST)[None, :]
    f32, bf16 = jnp.float32, jnp.bfloat16

    scatter_scratch = (
        [pltpu.VMEM((n, depth, width), f32)] * 2
        + [pltpu.VMEM((n // 2, depth, width), bf16)] * 8
        + [pltpu.SemaphoreType.DMA((2, steps + 1, 2))]
    )
    gather_scratch = [pltpu.VMEM((n, depth, width), bf16)] * 2 + [
        pltpu.VMEM((columns, rows), f32),
        pltpu.VMEM((steps + 1, columns, columns), f32),
        pltpu.VMEM((steps, columns, columns), f32),
        pltpu.SemaphoreType.DMA((2, 2 * steps, 2)),
        pltpu.SemaphoreType.DMA((2, steps)),
    ]
    vmem = pl.BlockSpec(memory_space=pltpu.VMEM)
    flops = 2 * rows * params * columns
    product_shapes = (
        jax.ShapeDtypeStruct((columns, rows), f32),
        jax.ShapeDtypeStruct((columns, columns), f32),
    )

    def call(kernel, number, shapes, scratch, *operands):
        return pl.pallas_call(
            kernel,
            out_shape=shapes,
            in_specs=[pl.BlockSpec(memory_space=pl.ANY)] + [vmem] * (len(operands) - 1),
            out_specs=jax.tree.map(lambda _: vmem, shapes),
            scratch_shapes=[pltpu.VMEM((rows, params), bf16), pltpu.SemaphoreType.DMA((n,))] + scratch,
            cost_estimate=pl.CostEstimate(
                flops=flops, bytes_accessed=2 * rows * params, transcendentals=0
            ),
            compiler_params=pltpu.CompilerParams(
                collective_id=number, has_side_effects=True, vmem_limit_bytes=VMEM_LIMIT
            ),
        )(*operands)

    def orthonormal(sketched, gram):
        return pl.pallas_call(
            functools.partial(orthonormal_kernel, float(total_rows)),
            out_shape=(
                jax.ShapeDtypeStruct((columns, rows), f32),
                jax.ShapeDtypeStruct((columns, rows), bf16),
            ),
            in_specs=[vmem] * 3,
            out_specs=(vmem, vmem),
            scratch_shapes=[pltpu.VMEM((columns, columns), f32)],
        )(gram, sketched, weights)

    omega = smooth(sketch).astype(bf16).reshape(columns, width)
    first, gram = call(
        functools.partial(first_kernel, n), 0, product_shapes, gather_scratch, greens, omega, weights
    )
    _, weighted_one = orthonormal(first, gram)
    second, gram = call(
        functools.partial(second_kernel, n, scale), 1, product_shapes,
        scatter_scratch + gather_scratch, greens, weighted_one, weights,
    )
    basis, weighted_two = orthonormal(second, gram)
    projected = call(
        functools.partial(last_kernel, n, scale), 2,
        jax.ShapeDtypeStruct((columns, width), f32), scatter_scratch, greens, weighted_two,
    )
    coefficients = projected.reshape(sketch.shape).transpose(1, 2, 0)
    return (basis.T, coefficients)


def solution(mesh):
    in_specs = (P(("grp", "row"), None), P(("grp", "row")), P("grp"), P("grp", "row", None))
    out_specs = (P(("grp", "row"), None), P(("grp", "row"), None, None))
    return jax.shard_map(local, mesh=mesh, in_specs=in_specs, out_specs=out_specs, check_vma=False)
```
